32 devices in a mesh: sector: 8 (over z, y), mpo: 4 (over x, core).
Axes of the slice: x: 2, y: 2, z: 4, core: 2. Of those that a mesh axis runs over, the one named last changes fastest.
Arguments:
- guess: float32 [128, 128, 128], P('sector'), may hold values from -64 to 64
- diag_shift: float32 [128, 128, 128], P('sector'), may hold values from 0 to 6
- block_rows: int32 [128], P('sector'), may hold values from 64 to 128
- block_cols: int32 [128], P('sector'), may hold values from 64 to 128
- left_env: bfloat16 [64, 128, 128, 128], P('mpo', 'sector'), may hold values from -2 to 2
- right_env: bfloat16 [64, 128, 128, 128], P('mpo', 'sector'), may hold values from -2 to 2
- edge_input: int32 [256], P('sector'), may hold values from 0 to 15
- edge_left: int32 [256], P('sector'), may hold values from 0 to 15
- edge_right: int32 [256], P('sector'), may hold values from 0 to 15
- edge_owner: int32 [256, 1], P('sector'), may hold values from 0 to 7, as said below
- edge_slot: int32 [256], P('sector'), may hold values from 0 to 15, as said below
Outputs:
- images: float32 [3, 128, 128, 128], P(None, 'sector', 'mpo')
- next_basis: float32 [128, 128, 128], P('sector', 'mpo')
- ritz: float32 [3], replicated
The draws below stay inside these ranges and needn't reach their ends.
Inputs may be any that keep to these rules, and one draw needn't show every extreme that they name: `edge_owner`: among the 32 couplings of one index of sector, at most 8 name the same owner, and some owner is named by exactly 8. No coupling names the index of sector that holds it. `edge_slot`: couplings come in mirrored pairs: for every coupling e there is a coupling f with in_f = out_e and out_f = in_e.
All inputs are finite; a program needn't handle non-finite values.
Results may differ from the reference program's by a relative error of at most 0.025.
Values may be sent and summed in bfloat16 or wider, within the bound.
A program may use at most 64 MiB of HBM per device.

```python
import math
import jax
import jax.numpy as jnp
from jax import lax

P_SIZE = 128
W = 64
SLOT = 16
E_DEV = 32
LB = 16
APPLIES = 3
CAP = 8
BLOCKS = 128
EDGES = 256
ENVS = 128
N_SECTOR = 8
N_MPO = 4


def pair_tables(key):
    base_key = jax.random.fold_in(key, 7001)
    key_rounds, key_reorder, key_slots = jax.random.split(base_key, 3)
    rounds = N_SECTOR - 1
    shuffled = jax.random.permutation(key_rounds, rounds).astype(jnp.int32)
    position = jnp.arange(E_DEV, dtype=jnp.int32)
    picked_index = jnp.where(position < CAP, 0, 1 + (position - CAP) % (N_SECTOR - 2)).astype(jnp.int32)
    round_list = shuffled[picked_index]
    reorder = jax.random.permutation(key_reorder, E_DEV).astype(jnp.int32)
    round_list = round_list[reorder]
    device = jnp.arange(N_SECTOR, dtype=jnp.int32)[:, None]
    chosen = round_list[None, :]
    opposite = (chosen - device) % rounds
    partner = jnp.where(device == N_SECTOR - 1, chosen * (N_SECTOR // 2) % rounds, jnp.where(opposite == device, N_SECTOR - 1, opposite)).astype(jnp.int32)
    in_slots = jax.random.randint(key_slots, (N_SECTOR, E_DEV), 0, SLOT, dtype=jnp.int32)
    columns = jnp.broadcast_to(position[None, :], (N_SECTOR, E_DEV))
    partner_slots = in_slots[partner, columns]
    return (in_slots, partner, partner_slots)


def draw_edge_input(key, part):
    in_slots, partner, partner_slots = pair_tables(key)
    return in_slots.reshape(EDGES).astype(jnp.int32)


def draw_edge_owner(key, part):
    in_slots, partner, partner_slots = pair_tables(key)
    return partner.reshape(EDGES, 1).astype(jnp.int32)


def draw_edge_slot(key, part):
    in_slots, partner, partner_slots = pair_tables(key)
    return partner_slots.reshape(EDGES).astype(jnp.int32)


def draw_guess(key, part):
    base_key = jax.random.fold_in(key, 911)
    key_rows, key_cols, key_blocks, key_common, key_own = jax.random.split(base_key, 5)
    row_scale = jnp.exp(jax.random.uniform(key_rows, (P_SIZE,), jnp.float32, 0.0, 0.5 * math.log(10.0)))
    col_scale = jnp.exp(jax.random.uniform(key_cols, (P_SIZE,), jnp.float32, 0.0, 0.5 * math.log(10.0)))
    rising = 1.0 + 2.0 * jnp.arange(BLOCKS, dtype=jnp.float32) / (BLOCKS - 1)
    block_scale = jnp.exp(jax.random.uniform(key_blocks, (BLOCKS,), jnp.float32, 0.0, math.log(10.0)))
    common = jnp.clip(jax.random.normal(key_common, (P_SIZE, P_SIZE), jnp.float32), -4.0, 4.0)
    own_part = 0.6 * jnp.clip(jax.random.normal(key_own, (BLOCKS, P_SIZE, P_SIZE), jnp.float32), -4.0, 4.0)
    field = row_scale[:, None] * col_scale[None, :] * (common[None, :, :] + own_part)
    return ((rising * block_scale)[:, None, None] * field / 48.0).astype(jnp.float32)


def env_noise(key, shape):
    return jnp.clip(jax.random.normal(key, shape, jnp.float32), -4.0, 4.0)


def draw_left_env(key, part):
    base_key = jax.random.fold_in(key, 1301)
    key_match, key_amp, key_noise = jax.random.split(base_key, 3)
    group_size = W // N_MPO
    band_size = P_SIZE // N_MPO
    matching = jax.random.permutation(key_match, N_MPO).astype(jnp.int32)
    term_group = jnp.arange(W, dtype=jnp.int32) // group_size
    row_band = jnp.arange(P_SIZE, dtype=jnp.int32) // band_size
    strong = (matching[term_group][:, None] == row_band[None, :]).astype(jnp.float32)
    amplitude = jax.random.uniform(key_amp, (W, ENVS, P_SIZE), jnp.float32, 0.5, 1.5) * (2.0 / group_size) * strong[:, None, :]
    noise = env_noise(key_noise, (W, ENVS, P_SIZE, P_SIZE)) * (0.6 / math.sqrt(W * P_SIZE))
    on_diagonal = jnp.arange(P_SIZE, dtype=jnp.int32)[:, None] == jnp.arange(P_SIZE, dtype=jnp.int32)[None, :]
    values = noise + jnp.where(on_diagonal, amplitude[:, :, :, None], 0.0)
    return values.astype(jnp.bfloat16)


def draw_right_env(key, part):
    base_key = jax.random.fold_in(key, 1709)
    key_amp, key_noise = jax.random.split(base_key, 2)
    amplitude = jax.random.uniform(key_amp, (W, ENVS, P_SIZE), jnp.float32, 0.5, 1.5)
    noise = env_noise(key_noise, (W, ENVS, P_SIZE, P_SIZE)) * (0.3 / math.sqrt(P_SIZE))
    on_diagonal = jnp.arange(P_SIZE, dtype=jnp.int32)[:, None] == jnp.arange(P_SIZE, dtype=jnp.int32)[None, :]
    values = noise + jnp.where(on_diagonal, amplitude[:, :, :, None], 0.0)
    return values.astype(jnp.bfloat16)


def set_ends(entries, key, low, largest):
    longest = entries.shape.index(max(entries.shape))
    spots = []
    for shift in (0, 1):
        where = [jax.random.randint(jax.random.fold_in(key, axis), (), 0, length) for axis, length in enumerate(entries.shape)]
        where[longest] = (where[longest] + shift) % entries.shape[longest]
        spots.append(tuple(where))
    return entries.at[spots[0]].set(low).at[spots[1]].set(largest)


def shard_levels(stream_key, shape, shards, least, largest):
    loudness = 1.0
    for dim, shards_of in shards:
        heights = jax.random.uniform(jax.random.fold_in(jax.random.fold_in(stream_key, 6), dim), (shards_of,), jnp.float32, least / len(shards), largest / len(shards))
        loudness = loudness * jnp.repeat(jnp.exp(heights), shape[dim] // shards_of).reshape((-1,) + (1,) * (len(shape) - 1 - dim))
    return loudness


def setup_inputs(seed: int = 0) -> dict:
    splits = jax.random.split(jax.random.key(seed), 12)
    guess = draw_guess(jax.random.fold_in(splits[11], 71), 0)
    diag_shift = jnp.clip(6.0 * jax.random.uniform(splits[1], (BLOCKS, P_SIZE, P_SIZE), jnp.float32) ** shard_levels(splits[1], (BLOCKS, P_SIZE, P_SIZE), ((0, 8),), -0.2, 0.2), 0.0, 6.0)
    block_rows = set_ends(jax.random.randint(splits[2], (BLOCKS,), P_SIZE // 2, P_SIZE + 1), jax.random.fold_in(splits[2], 1), P_SIZE // 2, P_SIZE).astype(jnp.int32)
    block_cols = set_ends(jax.random.randint(splits[3], (BLOCKS,), P_SIZE // 2, P_SIZE + 1), jax.random.fold_in(splits[3], 1), P_SIZE // 2, P_SIZE).astype(jnp.int32)
    left_env = draw_left_env(jax.random.fold_in(splits[11], 71), 0)
    right_env = draw_right_env(jax.random.fold_in(splits[11], 71), 0)
    edge_input = draw_edge_input(jax.random.fold_in(splits[11], 71), 0)
    edge_left = set_ends(jax.random.randint(splits[7], (EDGES,), 0, LB), jax.random.fold_in(splits[7], 1), 0, LB - 1).astype(jnp.int32)
    edge_right = set_ends(jax.random.randint(splits[8], (EDGES,), 0, LB), jax.random.fold_in(splits[8], 1), 0, LB - 1).astype(jnp.int32)
    edge_owner = draw_edge_owner(jax.random.fold_in(splits[11], 71), 0)
    edge_slot = draw_edge_slot(jax.random.fold_in(splits[11], 71), 0)
    return {"guess": guess, "diag_shift": diag_shift, "block_rows": block_rows, "block_cols": block_cols, "left_env": left_env, "right_env": right_env, "edge_input": edge_input, "edge_left": edge_left, "edge_right": edge_right, "edge_owner": edge_owner, "edge_slot": edge_slot}


def coupling_terms(xin, left_env, right_env, in_global, left_global, right_global):
    group = W // N_MPO
    left_groups = left_env.reshape(N_MPO, group, ENVS, P_SIZE, P_SIZE)
    right_groups = right_env.reshape(N_MPO, group, ENVS, P_SIZE, P_SIZE)

    def one_block(indices):
        inputs, lefts, rights = indices
        picked = xin[inputs].astype(jnp.float32)

        def one_group(envs):
            left_group, right_group = envs

            def one_term(total, pair):
                left_term, right_term = pair
                half = jnp.einsum('eij,ejk->eik', picked, right_term[rights].astype(jnp.float32))
                half = half.astype(jnp.bfloat16).astype(jnp.float32)
                return (total + jnp.einsum('eij,ejk->eik', left_term[lefts].astype(jnp.float32), half), None)
            total, _ = lax.scan(one_term, jnp.zeros((E_DEV, P_SIZE, P_SIZE), jnp.float32), (left_group, right_group))
            return total.astype(jnp.bfloat16)
        parts = lax.map(one_group, (left_groups, right_groups))
        return lax.optimization_barrier(jnp.sum(parts.astype(jnp.float32), axis=0)).astype(jnp.bfloat16)
    blocks = lax.map(one_block, (in_global.reshape(N_SECTOR, E_DEV), left_global.reshape(N_SECTOR, E_DEV), right_global.reshape(N_SECTOR, E_DEV)))
    return blocks.reshape(EDGES, P_SIZE, P_SIZE)

def reference(guess, diag_shift, block_rows, block_cols, left_env, right_env, edge_input, edge_left, edge_right, edge_owner, edge_slot):
    rows_index = lax.broadcasted_iota(jnp.int32, (BLOCKS, P_SIZE, P_SIZE), 1)
    cols_index = lax.broadcasted_iota(jnp.int32, (BLOCKS, P_SIZE, P_SIZE), 2)
    mask = ((rows_index < block_rows[:, None, None]) & (cols_index < block_cols[:, None, None])).astype(jnp.float32)
    source = (jnp.arange(EDGES, dtype=jnp.int32) // E_DEV).astype(jnp.int32)
    in_global = (source * SLOT + edge_input).astype(jnp.int32)
    left_global = (source * LB + edge_left).astype(jnp.int32)
    right_global = (source * LB + edge_right).astype(jnp.int32)
    out_global = (edge_owner[:, 0] * SLOT + edge_slot).astype(jnp.int32)
    start = mask * guess
    basis = [start / jnp.sqrt(jnp.sum(start * start) + 1e-06)]
    image_list = []
    ritz_list = []
    for step in range(APPLIES):
        current = basis[-1]
        xin = current.astype(jnp.bfloat16)
        contrib = coupling_terms(xin, left_env, right_env, in_global, left_global, right_global)
        image = jax.ops.segment_sum(contrib.astype(jnp.float32), out_global, num_segments=BLOCKS) * mask
        image_list.append(image)
        theta = jnp.sum(current * image)
        ritz_list.append(theta)
        corr = mask * (image - theta * current) / jnp.maximum(jnp.abs(diag_shift - theta), 1.0)
        ortho = corr
        for vector in basis:
            ortho = ortho - jnp.sum(vector * corr) * vector
        basis.append(ortho / jnp.sqrt(jnp.sum(ortho * ortho) + 1e-06))
    return (jnp.stack(image_list), basis[-1], jnp.stack(ritz_list))
```

```python
import functools

import jax
import jax.numpy as jnp
from jax import lax
from jax.experimental import pallas as pl
from jax.experimental.pallas import tpu as pltpu
from jax.sharding import PartitionSpec as P

APPLIES = 3
CHUNKS = 4
GROUP = 4
MESH = pl.DeviceIdType.MESH


def davidson_kernel(
    sectors,
    ranks,
    capacity,
    in_ref,
    left_ref,
    right_ref,
    source_ref,
    perm_ref,
    keep_ref,
    last_ref,
    has_ref,
    start_ref,
    mask_ref,
    diag_ref,
    lenv_hbm,
    renv_hbm,
    images_ref,
    next_ref,
    ritz_ref,
    lenv,
    renv,
    basis,
    gathered,
    parts,
    part_in,
    total,
    packed,
    arrived,
    running,
    gram,
    sum_m,
    sum_s,
    env_sem,
    x_send,
    x_recv,
    p_send,
    p_recv,
    a_send,
    a_recv,
    sm_send,
    sm_recv,
    ss_send,
    ss_recv,
):
    terms, _, size, _ = lenv.shape
    slots, share, _ = mask_ref.shape
    edges = in_ref.shape[0]
    per_chunk = edges // CHUNKS
    sec = lax.axis_index("sector")
    me = lax.axis_index("mpo")
    m_peers = [lax.rem(me + d, ranks) for d in range(1, ranks)]
    s_peers = [lax.rem(sec + d, sectors) for d in range(1, sectors)]

    lcopy = pltpu.make_async_copy(lenv_hbm, lenv, env_sem.at[0])
    rcopy = pltpu.make_async_copy(renv_hbm, renv, env_sem.at[1])
    rcopy.start()
    lcopy.start()

    barrier = pltpu.get_barrier_semaphore()
    for peer in m_peers:
        pl.semaphore_signal(barrier, inc=1, device_id=(sec, peer), device_id_type=MESH)
    for peer in s_peers:
        pl.semaphore_signal(barrier, inc=1, device_id=(peer, me), device_id_type=MESH)
    pl.semaphore_wait(barrier, ranks + sectors - 2)

    def to_rank(src, dst, send, recv, peer):
        return pltpu.make_async_remote_copy(
            src_ref=src, dst_ref=dst, send_sem=send, recv_sem=recv,
            device_id=(sec, peer), device_id_type=MESH,
        )

    def to_sector(src, dst, send, recv, peer):
        return pltpu.make_async_remote_copy(
            src_ref=src, dst_ref=dst, send_sem=send, recv_sem=recv,
            device_id=(peer, me), device_id_type=MESH,
        )

    def fold(value):
        return jnp.sum(value.reshape(slots * share, size), axis=0, keepdims=True)

    def add_up(index, rows):
        filler = [jnp.zeros((8 - len(rows), size), jnp.float32)] if len(rows) < 8 else []
        sum_m[index, me] = jnp.concatenate(rows + filler, axis=0)
        for peer in m_peers:
            to_rank(sum_m.at[index, me], sum_m.at[index, me],
                    sm_send.at[index, peer], sm_recv.at[index, me], peer).start()
        for peer in m_peers:
            to_rank(sum_m.at[index, peer], sum_m.at[index, peer],
                    sm_send.at[index, peer], sm_recv.at[index, peer], peer).wait()
        value = sum_m[index, 0]
        for i in range(1, ranks):
            value = value + sum_m[index, i]
        sum_s[index, sec] = value
        for peer in s_peers:
            to_sector(sum_s.at[index, sec], sum_s.at[index, sec],
                      ss_send.at[index, peer], ss_recv.at[index, sec], peer).start()
        for peer in s_peers:
            to_sector(sum_s.at[index, peer], sum_s.at[index, peer],
                      ss_send.at[index, peer], ss_recv.at[index, peer], peer).wait()
        value = sum_s[index, 0]
        for i in range(1, sectors):
            value = value + sum_s[index, i]
        return jnp.sum(value, axis=1, keepdims=True)

    first = pl.multiple_of(me * share, share)
    own_start = start_ref[:, pl.ds(first, share), :]
    norm = add_up(0, [fold(own_start * own_start)])[0:1, :]
    scale = 1.0 / jnp.sqrt(norm + 1e-06)
    basis[0] = own_start * scale[None]
    for j in range(1, APPLIES + 1):
        basis[j] = jnp.zeros((slots, share, size), jnp.float32)
    for m in range(ranks):
        gathered[0, m] = (
            start_ref[:, m * share:(m + 1) * share, :] * scale[None]
        ).astype(jnp.bfloat16)
    gram[...] = jnp.zeros_like(gram)
    for k in range(APPLIES):
        arrived[k, pl.ds(sec * capacity, capacity)] = jnp.zeros(
            (capacity, share, size), jnp.bfloat16)
    rcopy.wait()
    lcopy.wait()

    def apply(k, carry):
        @pl.when(k > 0)
        def _():
            for peer in m_peers:
                to_rank(gathered.at[k, peer], gathered.at[k, peer],
                        x_send.at[k, peer], x_recv.at[k, peer], peer).wait()

        def one_edge(e, carry):
            a, l, r = in_ref[e], left_ref[e], right_ref[e]
            x = jnp.concatenate([gathered[k, m, a] for m in range(ranks)], axis=0)
            acc = jnp.zeros((size, size), jnp.float32)
            for w in range(0, terms, GROUP):
                halves = []
                for v in range(w, w + GROUP, 2):
                    pair = jnp.concatenate([renv[v, r], renv[v + 1, r]], axis=1)
                    h = jnp.dot(x, pair, preferred_element_type=jnp.float32)
                    h = h.astype(jnp.bfloat16)
                    halves += [h[:, :size], h[:, size:]]
                half = jnp.concatenate(halves, axis=0)
                lefts = jnp.concatenate([lenv[v, l] for v in range(w, w + GROUP)], axis=1)
                acc = acc + jnp.dot(lefts, half, preferred_element_type=jnp.float32)
            out = acc.astype(jnp.bfloat16)
            for m in range(ranks):
                parts[k, m, e] = out[m * share:(m + 1) * share]
            return carry

        def part_copy(c, peer, slot):
            rows = pl.ds(c * per_chunk, per_chunk)
            return to_rank(parts.at[k, peer, rows], part_in.at[k, slot, rows],
                           p_send.at[k, c, peer], p_recv.at[k, c, slot], peer)

        def rank_range(c):
            done = [(c + 1) * per_chunk // (sectors - 1), c * per_chunk // (sectors - 1)]
            low, high = min(done[1], capacity), min(done[0], capacity)
            return (low, capacity) if c == CHUNKS - 1 else (low, high)

        def block_copy(c, peer, slot):
            low, high = rank_range(c)
            count = high - low
            return to_sector(packed.at[k, pl.ds(peer * capacity + low, count)],
                             arrived.at[k, pl.ds(slot * capacity + low, count)],
                             a_send.at[k, c, peer], a_recv.at[k, c, slot], peer)

        def finish(c):
            for peer in m_peers:
                part_copy(c, peer, peer).wait()
            rows = pl.ds(c * per_chunk, per_chunk)
            value = parts[k, me, rows].astype(jnp.float32)
            for peer in m_peers:
                value = value + part_in[k, peer, rows].astype(jnp.float32)
            total[k, rows] = value.astype(jnp.bfloat16)
            low, high = rank_range(c)
            if high > low:
                for peer in s_peers:
                    for i in range(low, high):
                        at = peer * capacity + i
                        packed[k, at] = total[k, source_ref[at]]
                    block_copy(c, peer, sec).start()

        for c in range(CHUNKS):
            lax.fori_loop(c * per_chunk, (c + 1) * per_chunk, one_edge, 0)
            for peer in m_peers:
                part_copy(c, peer, me).start()
            if c > 0:
                finish(c - 1)
        current = basis[k]
        gram_rows = [fold(current * basis[j]) for j in range(APPLIES)]
        finish(CHUNKS - 1)
        for c in range(CHUNKS):
            low, high = rank_range(c)
            if high > low:
                for peer in s_peers:
                    block_copy(c, peer, peer).wait()

        def take(t, acc):
            value = arrived[k, perm_ref[t]].astype(jnp.float32)
            acc = jnp.where(keep_ref[t] > 0, acc, 0.0) + value
            running[t] = acc
            return acc

        lax.fori_loop(0, (sectors - 1) * capacity, take, jnp.zeros((share, size), jnp.float32))
        for b in range(slots):
            block = running[last_ref[b]]
            images_ref[k, b] = jnp.where(has_ref[b] > 0, block, 0.0) * mask_ref[b]
        image = images_ref[k]
        current = basis[k]
        sums = add_up(1 + 2 * k, [fold(current * image)] + gram_rows)
        theta = sums[0:1, :]
        ritz_ref[k] = jnp.broadcast_to(theta, (8, size))
        gram[k] = jnp.broadcast_to(sums, (8, size))
        shift = theta[None]
        corr = mask_ref[...] * (image - shift * current) / jnp.maximum(
            jnp.abs(diag_ref[...] - shift), 1.0)
        sums = add_up(2 + 2 * k, [fold(corr * basis[j]) for j in range(APPLIES)]
                      + [fold(corr * corr)])
        proj = [sums[j:j + 1, :] for j in range(APPLIES)]
        length = sums[APPLIES:APPLIES + 1, :]
        ortho = corr
        for j in range(APPLIES):
            ortho = ortho - proj[j][None] * basis[j]
            length = length - 2.0 * proj[j] * proj[j]
        for i in range(APPLIES):
            for j in range(i + 1):
                inner = gram[i, 1 + j:2 + j, 0:1]
                times = 1.0 if i == j else 2.0
                length = length + times * proj[i] * proj[j] * inner
        new = ortho * (1.0 / jnp.sqrt(jnp.maximum(length, 0.0) + 1e-06))[None]
        basis[k + 1] = new

        @pl.when(k < APPLIES - 1)
        def _():
            gathered[k + 1, me] = new.astype(jnp.bfloat16)
            for peer in m_peers:
                to_rank(gathered.at[k + 1, me], gathered.at[k + 1, me],
                        x_send.at[k + 1, peer], x_recv.at[k + 1, me], peer).start()

        return carry

    lax.fori_loop(0, APPLIES, apply, 0)
    next_ref[...] = basis[APPLIES]


def per_device(
    guess,
    diag_shift,
    block_rows,
    block_cols,
    left_env,
    right_env,
    edge_input,
    edge_left,
    edge_right,
    edge_owner,
    edge_slot,
):
    slots, size, _ = guess.shape
    terms, envs, _, _ = left_env.shape
    sectors = lax.axis_size("sector")
    ranks = lax.axis_size("mpo")
    edges = edge_input.shape[0]
    capacity = max(2, 2 * edges // sectors)
    share = size // ranks
    first_row = lax.axis_index("mpo") * share
    places = sectors * capacity
    i32 = jnp.int32

    owner = edge_owner[:, 0]
    order = jnp.arange(edges, dtype=i32)
    earlier = (owner[:, None] == owner[None, :]) & (order[None, :] < order[:, None])
    rank = jnp.sum(earlier.astype(i32), axis=1)
    where_to = owner * capacity + rank
    hits = where_to[None, :] == jnp.arange(places, dtype=i32)[:, None]
    slot_ids = (jnp.sum(jnp.where(hits, edge_slot[None, :] + 1, 0), axis=1) - 1).reshape(
        sectors, capacity
    )
    key = rank * edges + order
    position = jnp.sum((key[None, :] < key[:, None]).astype(i32), axis=1)
    pick = position[None, :] == order[:, None]

    def sort_by(values):
        return jnp.sum(jnp.where(pick, values[None, :], 0), axis=1)

    source = jnp.sum(jnp.where(hits, position[None, :], 0), axis=1)

    ids = lax.all_to_all(slot_ids, "sector", split_axis=0, concat_axis=0, tiled=True).reshape(-1)
    place = jnp.arange(places, dtype=i32)
    ids = jnp.where(ids < 0, slots, ids)
    code = ids * places + place
    at = jnp.sum((code[None, :] < code[:, None]).astype(i32), axis=1)
    at_hits = at[None, :] == place[:, None]
    perm = jnp.sum(jnp.where(at_hits, place[None, :], 0), axis=1)
    sorted_ids = jnp.sum(jnp.where(at_hits, ids[None, :], 0), axis=1)
    keep = jnp.concatenate(
        [jnp.zeros((1,), i32), (sorted_ids[1:] == sorted_ids[:-1]).astype(i32)]
    )
    block = jnp.arange(slots, dtype=i32)
    upto = jnp.sum((ids[None, :] <= block[:, None]).astype(i32), axis=1)
    last = jnp.maximum(upto - 1, 0)
    has = jnp.max((ids[None, :] == block[:, None]).astype(i32), axis=1)

    rows_index = lax.broadcasted_iota(i32, guess.shape, 1)
    cols_index = lax.broadcasted_iota(i32, guess.shape, 2)
    mask = (
        (rows_index < block_rows[:, None, None]) & (cols_index < block_cols[:, None, None])
    ).astype(jnp.float32)
    start = mask * guess
    mask = lax.dynamic_slice_in_dim(mask, first_row, share, 1)
    diag = lax.dynamic_slice_in_dim(diag_shift, first_row, share, 1)

    f32, bf16 = jnp.float32, jnp.bfloat16
    sums = 1 + 2 * APPLIES
    dma = pltpu.SemaphoreType.DMA
    smem = pl.BlockSpec(memory_space=pltpu.SMEM)
    vmem = pl.BlockSpec(memory_space=pltpu.VMEM)
    hbm = pl.BlockSpec(memory_space=pl.ANY)
    images, final, ritz = pl.pallas_call(
        functools.partial(davidson_kernel, sectors, ranks, capacity),
        out_shape=(
            jax.ShapeDtypeStruct((APPLIES, slots, share, size), f32),
            jax.ShapeDtypeStruct((slots, share, size), f32),
            jax.ShapeDtypeStruct((APPLIES, 8, size), f32),
        ),
        in_specs=[smem] * 8 + [vmem] * 3 + [hbm] * 2,
        out_specs=(vmem, vmem, vmem),
        scratch_shapes=[
            pltpu.VMEM((terms, envs, size, size), bf16),
            pltpu.VMEM((terms, envs, size, size), bf16),
            pltpu.VMEM((APPLIES + 1, slots, share, size), f32),
            pltpu.VMEM((APPLIES, ranks, slots, share, size), bf16),
            pltpu.VMEM((APPLIES, ranks, edges, share, size), bf16),
            pltpu.VMEM((APPLIES, ranks, edges, share, size), bf16),
            pltpu.VMEM((APPLIES, edges, share, size), bf16),
            pltpu.VMEM((APPLIES, places, share, size), bf16),
            pltpu.VMEM((APPLIES, places, share, size), bf16),
            pltpu.VMEM((places, share, size), f32),
            pltpu.VMEM((APPLIES, 8, size), f32),
            pltpu.VMEM((sums, ranks, 8, size), f32),
            pltpu.VMEM((sums, sectors, 8, size), f32),
            dma((2,)),
            dma((APPLIES, ranks)),
            dma((APPLIES, ranks)),
            dma((APPLIES, CHUNKS, ranks)),
            dma((APPLIES, CHUNKS, ranks)),
            dma((APPLIES, CHUNKS, sectors)),
            dma((APPLIES, CHUNKS, sectors)),
            dma((sums, ranks)),
            dma((sums, ranks)),
            dma((sums, sectors)),
            dma((sums, sectors)),
        ],
        compiler_params=pltpu.CompilerParams(
            collective_id=0, has_side_effects=True, vmem_limit_bytes=56 * 1024 * 1024
        ),
        cost_estimate=pl.CostEstimate(
            flops=APPLIES * edges * terms * 4 * size**3,
            bytes_accessed=2 * terms * envs * size * size * 2,
            transcendentals=0,
        ),
        name="davidson",
    )(
        sort_by(edge_input),
        sort_by(edge_left),
        sort_by(edge_right),
        source,
        perm,
        keep,
        last,
        has,
        start,
        mask,
        diag,
        left_env,
        right_env,
    )
    return (images, final, ritz[:, 0, 0])


def solution(mesh):
    return jax.shard_map(
        per_device,
        mesh=mesh,
        in_specs=(
            P("sector", None, None),
            P("sector", None, None),
            P("sector"),
            P("sector"),
            P("mpo", "sector", None, None),
            P("mpo", "sector", None, None),
            P("sector"),
            P("sector"),
            P("sector"),
            P("sector", None),
            P("sector"),
        ),
        out_specs=(P(None, "sector", "mpo", None), P("sector", "mpo", None), P()),
        check_vma=False,
    )
```

```python
import functools

import jax
import jax.numpy as jnp
from jax import lax
from jax.experimental import pallas as pl
from jax.experimental.pallas import tpu as pltpu
from jax.sharding import PartitionSpec as P

APPLIES = 3
CHUNKS = 8
ABREAST = 2
GROUP = 4
MESH = pl.DeviceIdType.MESH


def davidson_kernel(
    sectors,
    ranks,
    capacity,
    in_ref,
    left_ref,
    right_ref,
    source_ref,
    rows_ref,
    cols_ref,
    ids_ref,
    guess_ref,
    diag_ref,
    lenv_hbm,
    renv_hbm,
    images_ref,
    next_ref,
    ritz_ref,
    lenv,
    renv,
    basis,
    gathered,
    parts,
    part_in,
    total,
    packed,
    arrived,
    ids,
    mask_ref,
    gram,
    sum_m,
    sum_s,
    env_sem,
    x_send,
    x_recv,
    p_send,
    p_recv,
    a_send,
    a_recv,
    sm_send,
    sm_recv,
    ss_send,
    ss_recv,
    id_send,
    id_recv,
):
    terms, _, size, _ = lenv.shape
    slots, share, _ = mask_ref.shape
    edges = in_ref.shape[0]
    per_chunk = edges // CHUNKS
    sec = lax.axis_index("sector")
    me = lax.axis_index("mpo")
    m_peers = [lax.rem(me + d, ranks) for d in range(1, ranks)]
    s_peers = [lax.rem(sec + d, sectors) for d in range(1, sectors)]

    lcopy = pltpu.make_async_copy(lenv_hbm, lenv, env_sem.at[0])
    rcopy = pltpu.make_async_copy(renv_hbm, renv, env_sem.at[1])
    rcopy.start()
    lcopy.start()

    barrier = pltpu.get_barrier_semaphore()
    for peer in m_peers:
        pl.semaphore_signal(barrier, inc=1, device_id=(sec, peer), device_id_type=MESH)
    for peer in s_peers:
        pl.semaphore_signal(barrier, inc=1, device_id=(peer, me), device_id_type=MESH)
    pl.semaphore_wait(barrier, ranks + sectors - 2)

    def to_rank(src, dst, send, recv, peer):
        return pltpu.make_async_remote_copy(
            src_ref=src, dst_ref=dst, send_sem=send, recv_sem=recv,
            device_id=(sec, peer), device_id_type=MESH,
        )

    def to_sector(src, dst, send, recv, peer):
        return pltpu.make_async_remote_copy(
            src_ref=src, dst_ref=dst, send_sem=send, recv_sem=recv,
            device_id=(peer, me), device_id_type=MESH,
        )

    def fold(value):
        return jnp.sum(value.reshape(slots * share, size), axis=0, keepdims=True)

    def add_up(index, rows):
        filler = [jnp.zeros((8 - len(rows), size), jnp.float32)] if len(rows) < 8 else []
        sum_m[index, me] = jnp.concatenate(rows + filler, axis=0)
        for peer in m_peers:
            to_rank(sum_m.at[index, me], sum_m.at[index, me],
                    sm_send.at[index, peer], sm_recv.at[index, me], peer).start()
        for peer in m_peers:
            to_rank(sum_m.at[index, peer], sum_m.at[index, peer],
                    sm_send.at[index, peer], sm_recv.at[index, peer], peer).wait()
        value = sum_m[index, 0]
        for i in range(1, ranks):
            value = value + sum_m[index, i]
        sum_s[index, sec] = value
        for peer in s_peers:
            to_sector(sum_s.at[index, sec], sum_s.at[index, sec],
                      ss_send.at[index, peer], ss_recv.at[index, sec], peer).start()
        for peer in s_peers:
            to_sector(sum_s.at[index, peer], sum_s.at[index, peer],
                      ss_send.at[index, peer], ss_recv.at[index, peer], peer).wait()
        value = sum_s[index, 0]
        for i in range(1, sectors):
            value = value + sum_s[index, i]
        return jnp.sum(value, axis=1, keepdims=True)

    def id_copy(peer, slot):
        return to_sector(ids_ref.at[pl.ds(peer * capacity, capacity)],
                         ids.at[pl.ds(slot * capacity, capacity)],
                         id_send.at[peer], id_recv.at[slot], peer)

    for peer in s_peers:
        id_copy(peer, sec).start()
    ids[pl.ds(sec * capacity, capacity)] = jnp.full((capacity, 8, size), -1, jnp.int32)

    first = pl.multiple_of(me * share, share)
    row = lax.broadcasted_iota(jnp.int32, (share, size), 0)
    col = lax.broadcasted_iota(jnp.int32, (share, size), 1)
    for b in range(slots):
        inside = (row + first < rows_ref[b]) & (col < cols_ref[b])
        mask_ref[b] = jnp.where(inside, 1.0, 0.0)
    own_start = guess_ref[:, pl.ds(first, share), :] * mask_ref[...]
    norm = add_up(0, [fold(own_start * own_start)])[0:1, :]
    scale = 1.0 / jnp.sqrt(norm + 1e-06)
    basis[0] = own_start * scale[None]
    for j in range(1, APPLIES + 1):
        basis[j] = jnp.zeros((slots, share, size), jnp.float32)
    for b in range(slots):
        for m in range(ranks):
            inside = (row + m * share < rows_ref[b]) & (col < cols_ref[b])
            part = guess_ref[b, m * share:(m + 1) * share, :]
            gathered[0, m, b] = (jnp.where(inside, part, 0.0) * scale).astype(jnp.bfloat16)
    gram[...] = jnp.zeros_like(gram)
    for k in range(APPLIES):
        arrived[k, pl.ds(sec * capacity, capacity)] = jnp.zeros(
            (capacity, share, size), jnp.bfloat16)
    for peer in s_peers:
        id_copy(peer, peer).wait()
    rcopy.wait()
    lcopy.wait()

    def apply(k, carry):
        @pl.when(k > 0)
        def _():
            for peer in m_peers:
                to_rank(gathered.at[k, peer], gathered.at[k, peer],
                        x_send.at[k, peer], x_recv.at[k, peer], peer).wait()

        def some_edges(edge_list):
            xs, lefts, rights = [], [], []
            for e in edge_list:
                a = in_ref[e]
                lefts.append(left_ref[e])
                rights.append(right_ref[e])
                xs.append(jnp.concatenate([gathered[k, m, a] for m in range(ranks)], axis=0))
            accs = [jnp.zeros((size, size), jnp.float32) for _ in edge_list]
            for w in range(0, terms, GROUP):
                halves = []
                for x, r in zip(xs, rights):
                    half = []
                    for v in range(w, w + GROUP, 2):
                        pair = jnp.concatenate([renv[v, r], renv[v + 1, r]], axis=1)
                        h = jnp.dot(x, pair, preferred_element_type=jnp.float32)
                        h = h.astype(jnp.bfloat16)
                        half += [h[:, :size], h[:, size:]]
                    halves.append(jnp.concatenate(half, axis=0))
                for i, l in enumerate(lefts):
                    wide = jnp.concatenate([lenv[v, l] for v in range(w, w + GROUP)], axis=1)
                    accs[i] = accs[i] + jnp.dot(
                        wide, halves[i], preferred_element_type=jnp.float32)
            for e, acc in zip(edge_list, accs):
                out = acc.astype(jnp.bfloat16)
                for m in range(ranks):
                    parts[k, m, e] = out[m * share:(m + 1) * share]

        def part_copy(c, peer, slot):
            rows = pl.ds(c * per_chunk, per_chunk)
            return to_rank(parts.at[k, peer, rows], part_in.at[k, slot, rows],
                           p_send.at[k, c, peer], p_recv.at[k, c, slot], peer)

        def rank_range(c):
            low = min(c * per_chunk // (sectors - 1), capacity)
            high = min((c + 1) * per_chunk // (sectors - 1), capacity)
            return (low, capacity) if c == CHUNKS - 1 else (low, high)

        def block_copy(c, peer, slot):
            low, high = rank_range(c)
            count = high - low
            return to_sector(packed.at[k, pl.ds(peer * capacity + low, count)],
                             arrived.at[k, pl.ds(slot * capacity + low, count)],
                             a_send.at[k, c, peer], a_recv.at[k, c, slot], peer)

        def add_parts(c):
            for peer in m_peers:
                part_copy(c, peer, peer).wait()
            rows = pl.ds(c * per_chunk, per_chunk)
            value = parts[k, me, rows].astype(jnp.float32)
            for peer in m_peers:
                value = value + part_in[k, peer, rows].astype(jnp.float32)
            total[k, rows] = value.astype(jnp.bfloat16)

        def send_blocks(c):
            low, high = rank_range(c)
            for peer in s_peers:
                for i in range(low, high):
                    at = peer * capacity + i
                    packed[k, at] = total[k, source_ref[at]]
                block_copy(c, peer, sec).start()

        sending = [c for c in range(CHUNKS) if rank_range(c)[1] > rank_range(c)[0]]

        def chunk(c, carry):
            for i in range(0, per_chunk, ABREAST):
                some_edges([c * per_chunk + i + j for j in range(ABREAST)])
            for peer in m_peers:
                part_copy(c, peer, me).start()

            @pl.when(c > 0)
            def _():
                add_parts(c - 1)

            for s in sending:
                if s < CHUNKS - 1:
                    pl.when(c == s + 1)(functools.partial(send_blocks, s))
            return carry

        lax.fori_loop(0, CHUNKS, chunk, 0)
        current = basis[k]
        gram_rows = [fold(current * basis[j]) for j in range(APPLIES)]
        add_parts(CHUNKS - 1)
        if CHUNKS - 1 in sending:
            send_blocks(CHUNKS - 1)
        for c in sending:
            for peer in s_peers:
                block_copy(c, peer, peer).wait()

        for low in range(0, slots, 8):
            count = min(8, slots - low)

            def take(t, accs):
                value = arrived[k, t].astype(jnp.float32).reshape(share // 8, 8, size)
                tag = ids[t]
                return tuple(
                    acc + jnp.where((tag == low + b)[None], value, 0.0)
                    for b, acc in enumerate(accs)
                )

            zero = jnp.zeros((share // 8, 8, size), jnp.float32)
            accs = lax.fori_loop(0, sectors * capacity, take, (zero,) * count, unroll=2)
            for b in range(count):
                images_ref[k, low + b] = accs[b].reshape(share, size) * mask_ref[low + b]
        image = images_ref[k]
        current = basis[k]
        sums = add_up(1 + 2 * k, [fold(current * image)] + gram_rows)
        theta = sums[0:1, :]
        ritz_ref[k] = jnp.broadcast_to(theta, (8, size))
        gram[k] = jnp.broadcast_to(sums, (8, size))
        shift = theta[None]
        corr = mask_ref[...] * (image - shift * current) / jnp.maximum(
            jnp.abs(diag_ref[:, pl.ds(first, share), :] - shift), 1.0)
        sums = add_up(2 + 2 * k, [fold(corr * basis[j]) for j in range(APPLIES)]
                      + [fold(corr * corr)])
        proj = [sums[j:j + 1, :] for j in range(APPLIES)]
        length = sums[APPLIES:APPLIES + 1, :]
        ortho = corr
        for j in range(APPLIES):
            ortho = ortho - proj[j][None] * basis[j]
            length = length - 2.0 * proj[j] * proj[j]
        for i in range(APPLIES):
            for j in range(i + 1):
                inner = gram[i, 1 + j:2 + j, 0:1]
                times = 1.0 if i == j else 2.0
                length = length + times * proj[i] * proj[j] * inner
        new = ortho * (1.0 / jnp.sqrt(jnp.maximum(length, 0.0) + 1e-06))[None]
        basis[k + 1] = new

        @pl.when(k < APPLIES - 1)
        def _():
            gathered[k + 1, me] = new.astype(jnp.bfloat16)
            for peer in m_peers:
                to_rank(gathered.at[k + 1, me], gathered.at[k + 1, me],
                        x_send.at[k + 1, peer], x_recv.at[k + 1, me], peer).start()

        return carry

    lax.fori_loop(0, APPLIES, apply, 0)
    next_ref[...] = basis[APPLIES]


def per_device(
    guess,
    diag_shift,
    block_rows,
    block_cols,
    left_env,
    right_env,
    edge_input,
    edge_left,
    edge_right,
    edge_owner,
    edge_slot,
):
    slots, size, _ = guess.shape
    terms, envs, _, _ = left_env.shape
    sectors = lax.axis_size("sector")
    ranks = lax.axis_size("mpo")
    edges = edge_input.shape[0]
    capacity = max(2, 2 * edges // sectors)
    share = size // ranks
    places = sectors * capacity
    i32 = jnp.int32

    owner = edge_owner[:, 0]
    order = jnp.arange(edges, dtype=i32)
    earlier = (owner[:, None] == owner[None, :]) & (order[None, :] < order[:, None])
    rank = jnp.sum(earlier.astype(i32), axis=1)
    where_to = owner * capacity + rank
    hits = where_to[None, :] == jnp.arange(places, dtype=i32)[:, None]
    slot_ids = jnp.sum(jnp.where(hits, edge_slot[None, :] + 1, 0), axis=1) - 1
    key = rank * edges + order
    position = jnp.sum((key[None, :] < key[:, None]).astype(i32), axis=1)
    pick = position[None, :] == order[:, None]

    tables = jnp.stack([edge_input, edge_left, edge_right])
    tables = jnp.sum(jnp.where(pick[None], tables[:, None, :], 0), axis=2)
    source = jnp.sum(jnp.where(hits, position[None, :], 0), axis=1)
    ids = jnp.broadcast_to(slot_ids[:, None, None], (places, 8, size))

    f32, bf16 = jnp.float32, jnp.bfloat16
    sums = 1 + 2 * APPLIES
    dma = pltpu.SemaphoreType.DMA
    smem = pl.BlockSpec(memory_space=pltpu.SMEM)
    vmem = pl.BlockSpec(memory_space=pltpu.VMEM)
    hbm = pl.BlockSpec(memory_space=pl.ANY)
    images, final, ritz = pl.pallas_call(
        functools.partial(davidson_kernel, sectors, ranks, capacity),
        out_shape=(
            jax.ShapeDtypeStruct((APPLIES, slots, share, size), f32),
            jax.ShapeDtypeStruct((slots, share, size), f32),
            jax.ShapeDtypeStruct((APPLIES, 8, size), f32),
        ),
        in_specs=[smem] * 6 + [vmem] * 3 + [hbm] * 2,
        out_specs=(vmem, vmem, vmem),
        scratch_shapes=[
            pltpu.VMEM((terms, envs, size, size), bf16),
            pltpu.VMEM((terms, envs, size, size), bf16),
            pltpu.VMEM((APPLIES + 1, slots, share, size), f32),
            pltpu.VMEM((APPLIES, ranks, slots, share, size), bf16),
            pltpu.VMEM((APPLIES, ranks, edges, share, size), bf16),
            pltpu.VMEM((APPLIES, ranks, edges, share, size), bf16),
            pltpu.VMEM((APPLIES, edges, share, size), bf16),
            pltpu.VMEM((APPLIES, places, share, size), bf16),
            pltpu.VMEM((APPLIES, places, share, size), bf16),
            pltpu.VMEM((places, 8, size), i32),
            pltpu.VMEM((slots, share, size), f32),
            pltpu.VMEM((APPLIES, 8, size), f32),
            pltpu.VMEM((sums, ranks, 8, size), f32),
            pltpu.VMEM((sums, sectors, 8, size), f32),
            dma((2,)),
            dma((APPLIES, ranks)),
            dma((APPLIES, ranks)),
            dma((APPLIES, CHUNKS, ranks)),
            dma((APPLIES, CHUNKS, ranks)),
            dma((APPLIES, CHUNKS, sectors)),
            dma((APPLIES, CHUNKS, sectors)),
            dma((sums, ranks)),
            dma((sums, ranks)),
            dma((sums, sectors)),
            dma((sums, sectors)),
            dma((sectors,)),
            dma((sectors,)),
        ],
        compiler_params=pltpu.CompilerParams(
            collective_id=0, has_side_effects=True, vmem_limit_bytes=56 * 1024 * 1024
        ),
        cost_estimate=pl.CostEstimate(
            flops=APPLIES * edges * terms * 4 * size**3,
            bytes_accessed=2 * terms * envs * size * size * 2,
            transcendentals=0,
        ),
        name="davidson",
    )(
        tables[0],
        tables[1],
        tables[2],
        source,
        block_rows,
        block_cols,
        ids,
        guess,
        diag_shift,
        left_env,
        right_env,
    )
    return (images, final, ritz[:, 0, 0])


def solution(mesh):
    return jax.shard_map(
        per_device,
        mesh=mesh,
        in_specs=(
            P("sector", None, None),
            P("sector", None, None),
            P("sector"),
            P("sector"),
            P("mpo", "sector", None, None),
            P("mpo", "sector", None, None),
            P("sector"),
            P("sector"),
            P("sector"),
            P("sector", None),
            P("sector"),
        ),
        out_specs=(P(None, "sector", "mpo", None), P("sector", "mpo", None), P()),
        check_vma=False,
    )
```

```python
import functools

import jax
import jax.numpy as jnp
from jax import lax
from jax.experimental import pallas as pl
from jax.experimental.pallas import tpu as pltpu
from jax.sharding import PartitionSpec as P

APPLIES = 3
CHUNKS = 8
ABREAST = 4
GROUP = 4
MESH = pl.DeviceIdType.MESH


def davidson_kernel(
    sectors,
    ranks,
    capacity,
    in_ref,
    left_ref,
    right_ref,
    source_ref,
    rows_ref,
    cols_ref,
    ids_ref,
    guess_ref,
    diag_ref,
    lenv_hbm,
    renv_hbm,
    images_ref,
    next_ref,
    ritz_ref,
    lenv,
    renv,
    basis,
    gathered,
    parts,
    part_in,
    total,
    packed,
    arrived,
    ids,
    mask_ref,
    gram,
    sum_m,
    sum_s,
    env_sem,
    x_send,
    x_recv,
    x_pass,
    p_send,
    p_recv,
    a_send,
    a_recv,
    sm_send,
    sm_recv,
    ss_send,
    ss_recv,
    id_send,
    id_recv,
):
    terms, _, size, _ = lenv.shape
    slots, share, _ = mask_ref.shape
    edges = in_ref.shape[0]
    per_chunk = edges // CHUNKS
    sec = lax.axis_index("sector")
    me = lax.axis_index("mpo")
    m_peers = [lax.rem(me + d, ranks) for d in range(1, ranks)]
    s_peers = [lax.rem(sec + d, sectors) for d in range(1, sectors)]

    lcopy = pltpu.make_async_copy(lenv_hbm, lenv, env_sem.at[0])
    rcopy = pltpu.make_async_copy(renv_hbm, renv, env_sem.at[1])
    rcopy.start()
    lcopy.start()

    barrier = pltpu.get_barrier_semaphore()
    for peer in m_peers:
        pl.semaphore_signal(barrier, inc=1, device_id=(sec, peer), device_id_type=MESH)
    for peer in s_peers:
        pl.semaphore_signal(barrier, inc=1, device_id=(peer, me), device_id_type=MESH)
    pl.semaphore_wait(barrier, ranks + sectors - 2)

    def to_rank(src, dst, send, recv, peer):
        return pltpu.make_async_remote_copy(
            src_ref=src, dst_ref=dst, send_sem=send, recv_sem=recv,
            device_id=(sec, peer), device_id_type=MESH,
        )

    def to_sector(src, dst, send, recv, peer):
        return pltpu.make_async_remote_copy(
            src_ref=src, dst_ref=dst, send_sem=send, recv_sem=recv,
            device_id=(peer, me), device_id_type=MESH,
        )

    partner = me + 1 - 2 * lax.rem(me, 2)
    alike = [lax.rem(me + d, ranks) for d in range(2, ranks, 2)]
    alike_across = [lax.rem(partner + d, ranks) for d in range(2, ranks, 2)]

    def x_copy(k, origin, peer, send):
        return to_rank(gathered.at[k, origin], gathered.at[k, origin],
                       send, x_recv.at[k, origin], peer)

    def fold(value):
        return jnp.sum(value.reshape(slots * share, size), axis=0, keepdims=True)

    def add_up(index, rows):
        filler = [jnp.zeros((8 - len(rows), size), jnp.float32)] if len(rows) < 8 else []
        sum_m[index, me] = jnp.concatenate(rows + filler, axis=0)
        for peer in m_peers:
            to_rank(sum_m.at[index, me], sum_m.at[index, me],
                    sm_send.at[index, peer], sm_recv.at[index, me], peer).start()
        for peer in m_peers:
            to_rank(sum_m.at[index, peer], sum_m.at[index, peer],
                    sm_send.at[index, peer], sm_recv.at[index, peer], peer).wait()
        value = sum_m[index, 0]
        for i in range(1, ranks):
            value = value + sum_m[index, i]
        sum_s[index, sec] = value
        for peer in s_peers:
            to_sector(sum_s.at[index, sec], sum_s.at[index, sec],
                      ss_send.at[index, peer], ss_recv.at[index, sec], peer).start()
        for peer in s_peers:
            to_sector(sum_s.at[index, peer], sum_s.at[index, peer],
                      ss_send.at[index, peer], ss_recv.at[index, peer], peer).wait()
        value = sum_s[index, 0]
        for i in range(1, sectors):
            value = value + sum_s[index, i]
        return jnp.sum(value, axis=1, keepdims=True)

    def id_copy(peer, slot):
        return to_sector(ids_ref.at[pl.ds(peer * capacity, capacity)],
                         ids.at[pl.ds(slot * capacity, capacity)],
                         id_send.at[peer], id_recv.at[slot], peer)

    for peer in s_peers:
        id_copy(peer, sec).start()
    ids[pl.ds(sec * capacity, capacity)] = jnp.full((capacity, 8, size), -1, jnp.int32)

    first = pl.multiple_of(me * share, share)
    row = lax.broadcasted_iota(jnp.int32, (share, size), 0)
    col = lax.broadcasted_iota(jnp.int32, (share, size), 1)
    for b in range(slots):
        inside = (row + first < rows_ref[b]) & (col < cols_ref[b])
        mask_ref[b] = jnp.where(inside, 1.0, 0.0)
    own_start = guess_ref[:, pl.ds(first, share), :] * mask_ref[...]
    norm = add_up(0, [fold(own_start * own_start)])[0:1, :]
    scale = 1.0 / jnp.sqrt(norm + 1e-06)
    basis[0] = own_start * scale[None]
    for j in range(1, APPLIES + 1):
        basis[j] = jnp.zeros((slots, share, size), jnp.float32)
    for b in range(slots):
        for m in range(ranks):
            inside = (row + m * share < rows_ref[b]) & (col < cols_ref[b])
            part = guess_ref[b, m * share:(m + 1) * share, :]
            gathered[0, m, b] = (jnp.where(inside, part, 0.0) * scale).astype(jnp.bfloat16)
    gram[...] = jnp.zeros_like(gram)
    for k in range(APPLIES):
        arrived[k, pl.ds(sec * capacity, capacity)] = jnp.zeros(
            (capacity, share, size), jnp.bfloat16)
    for peer in s_peers:
        id_copy(peer, peer).wait()
    rcopy.wait()
    lcopy.wait()

    def apply(k, carry):
        @pl.when(k > 0)
        def _():
            for peer in alike:
                x_copy(k, peer, peer, x_send.at[k, peer]).wait()
                x_copy(k, peer, partner, x_pass.at[k, peer]).start()
            x_copy(k, partner, partner, x_send.at[k, partner]).wait()
            for peer, across in zip(alike, alike_across):
                x_copy(k, peer, partner, x_pass.at[k, peer]).wait_send()
                x_copy(k, across, partner, x_pass.at[k, peer]).wait_recv()

        def some_edges(edge_list):
            xs, lefts, rights = [], [], []
            for e in edge_list:
                a = in_ref[e]
                lefts.append(left_ref[e])
                rights.append(right_ref[e])
                xs.append(jnp.concatenate([gathered[k, m, a] for m in range(ranks)], axis=0))
            accs = [jnp.zeros((size, size), jnp.float32) for _ in edge_list]
            for w in range(0, terms, GROUP):
                halves = []
                for x, r in zip(xs, rights):
                    half = []
                    for v in range(w, w + GROUP, 2):
                        pair = jnp.concatenate([renv[v, r], renv[v + 1, r]], axis=1)
                        h = jnp.dot(x, pair, preferred_element_type=jnp.float32)
                        h = h.astype(jnp.bfloat16)
                        half += [h[:, :size], h[:, size:]]
                    halves.append(jnp.concatenate(half, axis=0))
                for i, l in enumerate(lefts):
                    wide = jnp.concatenate([lenv[v, l] for v in range(w, w + GROUP)], axis=1)
                    accs[i] = accs[i] + jnp.dot(
                        wide, halves[i], preferred_element_type=jnp.float32)
            for e, acc in zip(edge_list, accs):
                out = acc.astype(jnp.bfloat16)
                for m in range(ranks):
                    parts[k, m, e] = out[m * share:(m + 1) * share]

        def part_copy(c, peer, slot):
            rows = pl.ds(c * per_chunk, per_chunk)
            return to_rank(parts.at[k, peer, rows], part_in.at[k, slot, rows],
                           p_send.at[k, c, peer], p_recv.at[k, c, slot], peer)

        def rank_range(c):
            low = min(c * per_chunk // (sectors - 1), capacity)
            high = min((c + 1) * per_chunk // (sectors - 1), capacity)
            return (low, capacity) if c == CHUNKS - 1 else (low, high)

        def block_copy(c, peer, slot):
            low, high = rank_range(c)
            count = high - low
            return to_sector(packed.at[k, pl.ds(peer * capacity + low, count)],
                             arrived.at[k, pl.ds(slot * capacity + low, count)],
                             a_send.at[k, c, peer], a_recv.at[k, c, slot], peer)

        def add_parts(c):
            for peer in m_peers:
                part_copy(c, peer, peer).wait()
            rows = pl.ds(c * per_chunk, per_chunk)
            value = parts[k, me, rows].astype(jnp.float32)
            for peer in m_peers:
                value = value + part_in[k, peer, rows].astype(jnp.float32)
            total[k, rows] = value.astype(jnp.bfloat16)

        def send_blocks(c):
            low, high = rank_range(c)
            for peer in s_peers:
                for i in range(low, high):
                    at = peer * capacity + i
                    packed[k, at] = total[k, source_ref[at]]
                block_copy(c, peer, sec).start()

        sending = [c for c in range(CHUNKS) if rank_range(c)[1] > rank_range(c)[0]]

        def chunk(c, carry):
            for i in range(0, per_chunk, ABREAST):
                some_edges([c * per_chunk + i + j for j in range(ABREAST)])
            for peer in m_peers:
                part_copy(c, peer, me).start()

            @pl.when(c > 0)
            def _():
                add_parts(c - 1)

            for s in sending:
                if s < CHUNKS - 1:
                    pl.when(c == s + 1)(functools.partial(send_blocks, s))
            return carry

        lax.fori_loop(0, CHUNKS, chunk, 0)
        current = basis[k]
        gram_rows = [fold(current * basis[j]) for j in range(APPLIES)]
        add_parts(CHUNKS - 1)
        if CHUNKS - 1 in sending:
            send_blocks(CHUNKS - 1)
        for c in sending:
            for peer in s_peers:
                block_copy(c, peer, peer).wait()

        for low in range(0, slots, 8):
            count = min(8, slots - low)

            def take(t, accs):
                value = arrived[k, t].astype(jnp.float32).reshape(share // 8, 8, size)
                tag = ids[t]
                return tuple(
                    acc + jnp.where((tag == low + b)[None], value, 0.0)
                    for b, acc in enumerate(accs)
                )

            zero = jnp.zeros((share // 8, 8, size), jnp.float32)
            accs = lax.fori_loop(0, sectors * capacity, take, (zero,) * count, unroll=2)
            for b in range(count):
                images_ref[k, low + b] = accs[b].reshape(share, size) * mask_ref[low + b]
        image = images_ref[k]
        current = basis[k]
        sums = add_up(1 + 2 * k, [fold(current * image)] + gram_rows)
        theta = sums[0:1, :]
        ritz_ref[k] = jnp.broadcast_to(theta, (8, size))
        gram[k] = jnp.broadcast_to(sums, (8, size))
        shift = theta[None]
        corr = mask_ref[...] * (image - shift * current) / jnp.maximum(
            jnp.abs(diag_ref[:, pl.ds(first, share), :] - shift), 1.0)
        sums = add_up(2 + 2 * k, [fold(corr * basis[j]) for j in range(APPLIES)]
                      + [fold(corr * corr)])
        proj = [sums[j:j + 1, :] for j in range(APPLIES)]
        length = sums[APPLIES:APPLIES + 1, :]
        ortho = corr
        for j in range(APPLIES):
            ortho = ortho - proj[j][None] * basis[j]
            length = length - 2.0 * proj[j] * proj[j]
        for i in range(APPLIES):
            for j in range(i + 1):
                inner = gram[i, 1 + j:2 + j, 0:1]
                times = 1.0 if i == j else 2.0
                length = length + times * proj[i] * proj[j] * inner
        new = ortho * (1.0 / jnp.sqrt(jnp.maximum(length, 0.0) + 1e-06))[None]
        basis[k + 1] = new

        @pl.when(k < APPLIES - 1)
        def _():
            gathered[k + 1, me] = new.astype(jnp.bfloat16)
            for peer in alike + [partner]:
                x_copy(k + 1, me, peer, x_send.at[k + 1, peer]).start()

        return carry

    lax.fori_loop(0, APPLIES, apply, 0)
    next_ref[...] = basis[APPLIES]


def per_device(
    guess,
    diag_shift,
    block_rows,
    block_cols,
    left_env,
    right_env,
    edge_input,
    edge_left,
    edge_right,
    edge_owner,
    edge_slot,
):
    slots, size, _ = guess.shape
    terms, envs, _, _ = left_env.shape
    sectors = lax.axis_size("sector")
    ranks = lax.axis_size("mpo")
    edges = edge_input.shape[0]
    capacity = max(2, 2 * edges // sectors)
    share = size // ranks
    places = sectors * capacity
    i32 = jnp.int32

    owner = edge_owner[:, 0]
    order = jnp.arange(edges, dtype=i32)
    earlier = (owner[:, None] == owner[None, :]) & (order[None, :] < order[:, None])
    rank = jnp.sum(earlier.astype(i32), axis=1)
    where_to = owner * capacity + rank
    hits = where_to[None, :] == jnp.arange(places, dtype=i32)[:, None]
    slot_ids = jnp.sum(jnp.where(hits, edge_slot[None, :] + 1, 0), axis=1) - 1
    key = rank * edges + order
    position = jnp.sum((key[None, :] < key[:, None]).astype(i32), axis=1)
    pick = position[None, :] == order[:, None]

    tables = jnp.stack([edge_input, edge_left, edge_right])
    tables = jnp.sum(jnp.where(pick[None], tables[:, None, :], 0), axis=2)
    source = jnp.sum(jnp.where(hits, position[None, :], 0), axis=1)
    ids = jnp.broadcast_to(slot_ids[:, None, None], (places, 8, size))

    f32, bf16 = jnp.float32, jnp.bfloat16
    sums = 1 + 2 * APPLIES
    dma = pltpu.SemaphoreType.DMA
    smem = pl.BlockSpec(memory_space=pltpu.SMEM)
    vmem = pl.BlockSpec(memory_space=pltpu.VMEM)
    hbm = pl.BlockSpec(memory_space=pl.ANY)
    images, final, ritz = pl.pallas_call(
        functools.partial(davidson_kernel, sectors, ranks, capacity),
        out_shape=(
            jax.ShapeDtypeStruct((APPLIES, slots, share, size), f32),
            jax.ShapeDtypeStruct((slots, share, size), f32),
            jax.ShapeDtypeStruct((APPLIES, 8, size), f32),
        ),
        in_specs=[smem] * 6 + [vmem] * 3 + [hbm] * 2,
        out_specs=(vmem, vmem, vmem),
        scratch_shapes=[
            pltpu.VMEM((terms, envs, size, size), bf16),
            pltpu.VMEM((terms, envs, size, size), bf16),
            pltpu.VMEM((APPLIES + 1, slots, share, size), f32),
            pltpu.VMEM((APPLIES, ranks, slots, share, size), bf16),
            pltpu.VMEM((APPLIES, ranks, edges, share, size), bf16),
            pltpu.VMEM((APPLIES, ranks, edges, share, size), bf16),
            pltpu.VMEM((APPLIES, edges, share, size), bf16),
            pltpu.VMEM((APPLIES, places, share, size), bf16),
            pltpu.VMEM((APPLIES, places, share, size), bf16),
            pltpu.VMEM((places, 8, size), i32),
            pltpu.VMEM((slots, share, size), f32),
            pltpu.VMEM((APPLIES, 8, size), f32),
            pltpu.VMEM((sums, ranks, 8, size), f32),
            pltpu.VMEM((sums, sectors, 8, size), f32),
            dma((2,)),
            dma((APPLIES, ranks)),
            dma((APPLIES, ranks)),
            dma((APPLIES, ranks)),
            dma((APPLIES, CHUNKS, ranks)),
            dma((APPLIES, CHUNKS, ranks)),
            dma((APPLIES, CHUNKS, sectors)),
            dma((APPLIES, CHUNKS, sectors)),
            dma((sums, ranks)),
            dma((sums, ranks)),
            dma((sums, sectors)),
            dma((sums, sectors)),
            dma((sectors,)),
            dma((sectors,)),
        ],
        compiler_params=pltpu.CompilerParams(
            collective_id=0, has_side_effects=True, vmem_limit_bytes=56 * 1024 * 1024
        ),
        cost_estimate=pl.CostEstimate(
            flops=APPLIES * edges * terms * 4 * size**3,
            bytes_accessed=2 * terms * envs * size * size * 2,
            transcendentals=0,
        ),
        name="davidson",
    )(
        tables[0],
        tables[1],
        tables[2],
        source,
        block_rows,
        block_cols,
        ids,
        guess,
        diag_shift,
        left_env,
        right_env,
    )
    return (images, final, ritz[:, 0, 0])


def solution(mesh):
    return jax.shard_map(
        per_device,
        mesh=mesh,
        in_specs=(
            P("sector", None, None),
            P("sector", None, None),
            P("sector"),
            P("sector"),
            P("mpo", "sector", None, None),
            P("mpo", "sector", None, None),
            P("sector"),
            P("sector"),
            P("sector"),
            P("sector", None),
            P("sector"),
        ),
        out_specs=(P(None, "sector", "mpo", None), P("sector", "mpo", None), P()),
        check_vma=False,
    )
```
